256 devices in a mesh: row: 32 (over x, z), col: 8 (over y, core).
Axes of the slice: x: 4, y: 4, z: 8, core: 2. Of those that a mesh axis runs over, the one named last changes fastest.
Arguments:
- front: float32 [2, 32, 256, 8, 8, 256], P(None, 'row', None, None, 'col'), as said below
- pattern: int32 [2, 32, 8, 8], P(None, 'row', None, 'col'), may hold values from 0 to 1, as said below
Outputs:
- factored: float32 [2, 32, 256, 8, 8, 256], P(None, 'row', None, None, 'col')
The draws below stay inside these ranges and needn't reach their ends.
Inputs may be any that keep to these rules, and one draw needn't show every extreme that they name: pattern is symmetric in blocks; block pairs at most two apart (the diagonal included) are always 1; for every k < 2, taken in order, block (i, j) with i > k and j > k is 1 wherever blocks (i, k) and (j, k) are both 1. front is symmetric and positive definite.
All inputs are finite; a program needn't handle non-finite values.
Results may differ from the reference program's by a relative error of at most 0.0001.
Values sent between devices are 32-bit elements; how exact they have to be, the bound alone decides.
No kernel may reach another device: no remote copies, remote signals or barrier semaphores. Data moves between devices by JAX's collectives and lax.ppermute only.
A program may use at most 64 MiB of HBM per device.

```python
import math
import jax
import jax.numpy as jnp
from jax import lax

B = 256
NBLK = 64
PANELS = 2
RB_DEV = 2
CB_DEV = 8
N_ROW = 32
N_COL = 8


def draw_pattern(key, part):
    key = jax.random.fold_in(key, 11)
    block_count = RB_DEV * N_ROW
    coin_draw = jax.random.randint(key, (block_count, block_count), 0, 16)
    positions = jnp.arange(block_count)
    banded = jnp.abs(positions[:, None] - positions[None, :]) <= 2
    extra_pairs = coin_draw == 0
    pattern_full = banded | extra_pairs | extra_pairs.T
    for column in range(PANELS):
        touched = pattern_full[:, column] & (positions > column)
        pattern_full = pattern_full | touched[:, None] & touched[None, :]
    return pattern_full.astype(jnp.int32).reshape(RB_DEV, N_ROW, CB_DEV, N_COL)


def draw_front(key, part):
    key = jax.random.fold_in(key, 23)
    point_key, rough_key, nugget_key, amplitude_key = jax.random.split(key, 4)
    block_count = RB_DEV * N_ROW
    matrix_order = block_count * B
    spots = jax.random.uniform(point_key, (3, matrix_order), jnp.float32)
    positions = jnp.arange(matrix_order)
    along = (positions // B).astype(jnp.float32) + spots[0]
    across = 4.0 * spots[1]
    depth = 4.0 * spots[2]
    gap_along = along[:, None] - along[None, :]
    gap_across = across[:, None] - across[None, :]
    gap_depth = depth[:, None] - depth[None, :]
    scaled = jnp.sqrt(gap_along * gap_along + gap_across * gap_across + gap_depth * gap_depth) * 0.5
    remaining = jnp.maximum(1.0 - scaled, 0.0)
    kernel = remaining * remaining * remaining * remaining * (4.0 * scaled + 1.0)
    entries = jnp.clip(jax.random.normal(rough_key, (matrix_order, matrix_order), jnp.float32), -4.0, 4.0)
    rough = (entries + entries.T) * (0.7071 * 0.45 / math.sqrt(matrix_order))
    nugget = 1.0 + 0.5 * jax.random.uniform(nugget_key, (matrix_order,), jnp.float32)
    inner = kernel + rough
    inner = inner.at[positions, positions].add(nugget)
    amplitude = jnp.exp(-3.0 * jax.random.uniform(amplitude_key, (matrix_order,), jnp.float32))
    symmetric = amplitude[:, None] * inner * amplitude[None, :]
    return symmetric.reshape(RB_DEV, N_ROW, B, CB_DEV, N_COL, B)


def setup_inputs(seed: int = 0) -> dict:
    key_list = jax.random.split(jax.random.key(seed), 3)
    front = draw_front(jax.random.fold_in(key_list[2], 71), 0)
    pattern = draw_pattern(jax.random.fold_in(key_list[2], 71), 0)
    return {"front": front, "pattern": pattern}


HIGHEST = lax.Precision.HIGHEST

def reference(front, pattern):
    block_count = NBLK
    block_width = B
    blocks = front.reshape(block_count, block_width, block_count, block_width).transpose(0, 2, 1, 3)
    present = pattern.reshape(block_count, block_count) > 0
    working = jnp.where(present[:, :, None, None], blocks, jnp.zeros((), blocks.dtype))
    block_index = jnp.arange(block_count, dtype=jnp.int32)
    identity = jnp.eye(block_width, dtype=jnp.float32)
    for column in range(PANELS):
        factor = jnp.linalg.cholesky(working[column, column])
        inverse = jax.scipy.linalg.solve_triangular(factor, identity, lower=True)
        panel_block = jnp.einsum('iab,cb->iac', working[:, column], inverse, precision=HIGHEST)
        panel_block = jnp.where((block_index == column)[:, None, None], factor[None], panel_block)
        panel_block = jnp.where((block_index < column)[:, None, None], jnp.zeros((), panel_block.dtype), panel_block)
        working = working.at[column:, column].set(panel_block[column:])
        working = working.at[column, column + 1:].set(jnp.transpose(panel_block[column + 1:], (0, 2, 1)))
        allowed_now = present & (block_index > column)[:, None] & (block_index > column)[None, :]

        def row_update(row_item):
            work_row, panel_row, allow_row = row_item
            product = jnp.einsum('ab,jcb->jac', panel_row, panel_block, precision=HIGHEST)
            return work_row - jnp.where(allow_row[:, None, None], product, jnp.zeros((), product.dtype))
        working = lax.map(row_update, (working, panel_block, allowed_now))
    return working.transpose(0, 2, 1, 3).reshape(RB_DEV, N_ROW, B, CB_DEV, N_COL, B)
```

```python
import jax
import jax.numpy as jnp
from jax import lax
from jax.experimental import pallas as pl
from jax.experimental.pallas import tpu as pltpu
from jax.sharding import PartitionSpec as P

W = 256
NB = 32
HIGHEST = lax.Precision.HIGHEST
F32 = jnp.float32
BF16 = jnp.bfloat16


def dot_nn(a, b):
    return lax.dot_general(a, b, (((1,), (0,)), ((), ())), precision=HIGHEST, preferred_element_type=F32)


def dot_nt(a, b):
    return lax.dot_general(a, b, (((1,), (1,)), ((), ())), precision=HIGHEST, preferred_element_type=F32)


def dot_tn(a, b):
    return lax.dot_general(a, b, (((0,), (0,)), ((), ())), precision=HIGHEST, preferred_element_type=F32)


def split3(x):
    hi = x.astype(BF16)
    rest = x - hi.astype(F32)
    mid = rest.astype(BF16)
    low = (rest - mid.astype(F32)).astype(BF16)
    return hi, mid, low


def eliminate(rows):
    sub = lax.broadcasted_iota(jnp.int32, (8, 384), 0)
    for t in range(4):
        x = rows[t]
        head = x[:, 0:128]
        cols = [jnp.broadcast_to(head[:, 8 * t + k : 8 * t + k + 1], (8, 128)) for k in range(8)]
        below = {
            g: [
                jnp.broadcast_to(rows[g][:, 8 * t + k : 8 * t + k + 1], (8, 128))
                for k in range(8)
            ]
            for g in range(t + 1, 4)
        }
        a = {
            (i, k): jnp.broadcast_to(cols[k][i : i + 1, :], (8, 128))
            for k in range(8)
            for i in range(k, 8)
        }
        r = [jnp.broadcast_to(x[k : k + 1, :], (8, 384)) for k in range(8)]
        for k in range(8):
            scale = lax.rsqrt(a[k, k])
            wide = jnp.concatenate([scale] * 3, axis=1)
            r[k] = r[k] * wide
            for g in below:
                below[g][k] = below[g][k] * scale
            l = {i: a[i, k] * scale for i in range(k + 1, 8)}
            for i in range(k + 1, 8):
                for j in range(k + 1, i + 1):
                    a[i, j] = a[i, j] - l[i] * l[j]
                r[i] = r[i] - jnp.concatenate([l[i]] * 3, axis=1) * r[k]
                for g in below:
                    below[g][i] = below[g][i] - l[i] * below[g][k]
        out = r[0]
        for k in range(1, 8):
            out = jnp.where(sub == k, r[k], out)
        rows[t] = out
        for g in below:
            acc = rows[g]
            for k in range(8):
                acc = acc - jnp.concatenate([below[g][k]] * 3, axis=1) * r[k]
            rows[g] = acc
    return rows


def factor_block(g_ref, u_ref, v_ref):
    lane = lax.broadcasted_iota(jnp.int32, (NB, W), 1)
    row = lax.broadcasted_iota(jnp.int32, (NB, W), 0)
    eye = (
        lax.broadcasted_iota(jnp.int32, (NB, 128), 0)
        == lax.broadcasted_iota(jnp.int32, (NB, 128), 1)
    ).astype(F32)
    tail = lax.broadcasted_iota(jnp.int32, (W - NB, W), 1)

    def panel(p, carry):
        x = jnp.concatenate([g_ref[0:NB, :], eye], axis=1)
        rows = eliminate([x[8 * t : 8 * t + 8] for t in range(4)])
        r = jnp.concatenate(rows, axis=0)
        shifted = pltpu.roll(r, 384 - NB, 1)[:, 0:W]
        at = pl.multiple_of(p * NB, NB)
        u_ref[pl.ds(at, NB), :] = jnp.where(
            lane >= row + at, pltpu.roll(r[:, 0:W], at, 1), 0.0
        )
        v_ref[pl.ds(at, NB), :] = jnp.where(
            lane <= row + at, pltpu.roll(shifted, at + NB, 1), 0.0
        )
        hi, mid, low = split3(shifted)
        left = jnp.concatenate([hi, hi, mid, mid, hi, low], axis=0)
        right = jnp.concatenate([hi, mid, hi, mid, low, hi], axis=0)
        prod = lax.dot_general(
            left, right, (((0,), (0,)), ((), ())), preferred_element_type=F32
        )
        old = pltpu.roll(g_ref[NB:W, :], W - NB, 1)
        g_ref[0 : W - NB, :] = jnp.where(tail < W - NB, old, 0.0) - prod[0 : W - NB, :]
        return carry

    lax.fori_loop(0, W // NB, panel, 0)


def factor_kernel(t_ref, a01_ref, u0_ref, v0_ref, pt_ref, u1_ref, v1_ref, g_ref):
    lower = lax.broadcasted_iota(jnp.int32, (W, W), 0)
    upper = lax.broadcasted_iota(jnp.int32, (W, W), 1)
    t = t_ref[0:W, :]
    flipped = jnp.transpose(t)
    g_ref[...] = jnp.where(lower >= upper, t, flipped)
    factor_block(g_ref, u0_ref, v0_ref)
    pt = dot_nn(v0_ref[...], a01_ref[0:W, :])
    pt_ref[...] = pt
    own = jnp.where(lower < upper, t, flipped)
    own = jnp.where(lower == upper, t_ref[W : W + 1, :], own)
    g_ref[...] = own - dot_tn(pt, pt)
    factor_block(g_ref, u1_ref, v1_ref)


def factor_pair(packed, a01):
    block = jax.ShapeDtypeStruct((W, W), F32)
    return pl.pallas_call(
        factor_kernel,
        out_shape=[block] * 5,
        scratch_shapes=[pltpu.VMEM((W, W), F32)],
        compiler_params=pltpu.CompilerParams(vmem_limit_bytes=32 * 1024 * 1024),
        name="factor_pair",
    )(packed, a01)


def extract_kernel(info_ref, front_ref, slab_ref, block_ref, *piece_refs):
    odd = info_ref[2]
    for m in range(2):
        keep = info_ref[m] > 0
        for h in range(2):
            part = front_ref[pl.ds(m * 4096 + h, W, stride=16), :]
            part = jnp.where(keep, part, 0.0)
            slab_ref[2 * m + h] = part
            if m == 0:
                block_ref[0:W, 128 * h : 128 * h + 128] = part
            for half in range(2):
                place = 2 * h + half
                mine = part[128 * half : 128 * half + 128]

                @pl.when(odd == 0)
                def _(place=place, mine=mine, m=m):
                    piece_refs[4 * m + place][...] = mine

                @pl.when(odd != 0)
                def _(place=place, mine=mine, m=m):
                    piece_refs[4 * (1 - m) + place][...] = mine

    block_ref[W : W + 8, :] = jnp.zeros((8, W), F32)


def extract(info, view):
    return pl.pallas_call(
        extract_kernel,
        in_specs=[
            pl.BlockSpec(memory_space=pltpu.SMEM),
            pl.BlockSpec(memory_space=pltpu.VMEM),
        ],
        out_specs=[pl.BlockSpec(memory_space=pltpu.VMEM)] * 10,
        out_shape=[
            jax.ShapeDtypeStruct((4, W, 128), F32),
            jax.ShapeDtypeStruct((W + 8, W), F32),
        ]
        + [jax.ShapeDtypeStruct((128, 128), F32)] * 8,
        compiler_params=pltpu.CompilerParams(vmem_limit_bytes=32 * 1024 * 1024),
        name="extract",
    )(info, view)


def split2(x):
    hi = x.astype(BF16)
    return hi, (x - hi.astype(F32)).astype(BF16)


def dot_bf(a, b):
    return lax.dot_general(a, b, (((1,), (1,)), ((), ())), preferred_element_type=F32)


def update_kernel(
    info_ref, mask_ref, front_ref, q_ref, p_ref, u0_ref, v0_ref, pt_ref, u1_ref, v1_ref,
    out_ref, qh_ref, ql_ref, ph_ref, pl_ref,
):
    step = pl.program_id(0)
    r, c, x = info_ref[0], info_ref[1], info_ref[2]
    lane = lax.broadcasted_iota(jnp.int32, (W, 2 * W), 1)
    row = lax.broadcasted_iota(jnp.int32, (W, 2 * W), 0)

    def solve(raw0, raw1, place):
        first = dot_nt(raw0, v0_ref[...])
        second = dot_nt(raw1 - dot_nn(first, pt_ref[...]), v1_ref[...])
        both = jnp.concatenate([first, second], axis=1)
        unit = jnp.where(lane == row + place * W, -1.0, 0.0)
        return split2(jnp.where(place < 2, unit, both))

    @pl.when(step == 0)
    def _():
        for m in range(2):
            raw = [
                jnp.concatenate([p_ref[s, 2 * m], p_ref[s, 2 * m + 1]], axis=1)
                for s in range(2)
            ]
            place = r if m == 0 else r + 32
            ph_ref[m], pl_ref[m] = solve(raw[0], raw[1], place)
        for n in range(8):
            m = n // 4
            near = lax.rem(n % 4 - x + 4, 4)
            raw = []
            for s in range(2):
                tall = []
                for h in range(2):
                    parts = [
                        q_ref[lax.rem(4 * m + 2 * h + half + c, 8), near, s]
                        for half in range(2)
                    ]
                    tall.append(jnp.concatenate(parts, axis=0))
                raw.append(jnp.concatenate(tall, axis=1))
            qh_ref[n], ql_ref[n] = solve(raw[0], raw[1], c + 8 * n)

    ph = ph_ref[step]
    pl_ = pl_ref[step]
    for n in range(8):
        qh = qh_ref[n]
        prod = dot_bf(ph, qh) + (dot_bf(ph, ql_ref[n]) + dot_bf(pl_, qh))
        keep = mask_ref[step, n] > 0
        for h in range(2):
            here = pl.ds(2 * n + h, W, stride=16)
            old = jnp.where(keep, front_ref[here, :], 0.0)
            out_ref[here, :] = old - prod[:, 128 * h : 128 * h + 128]

    def place_block(block):
        for h in range(2):
            out_ref[pl.ds(h, W, stride=16), :] = block[:, 128 * h : 128 * h + 128]

    corner = jnp.logical_and(step == 0, jnp.logical_and(r < 2, c < 2))

    @pl.when(jnp.logical_and(corner, r + c == 0))
    def _():
        place_block(jnp.transpose(u0_ref[...]))

    @pl.when(jnp.logical_and(corner, r < c))
    def _():
        place_block(pt_ref[...])

    @pl.when(jnp.logical_and(corner, r > c))
    def _():
        place_block(jnp.transpose(pt_ref[...]))

    @pl.when(jnp.logical_and(corner, r + c == 2))
    def _():
        place_block(jnp.transpose(u1_ref[...]))


def update(info, mask, view, gathered, rows, factors):
    whole = pl.BlockSpec(memory_space=pltpu.VMEM)
    return pl.pallas_call(
        update_kernel,
        grid=(2,),
        in_specs=[
            pl.BlockSpec(memory_space=pltpu.SMEM),
            pl.BlockSpec(memory_space=pltpu.SMEM),
            pl.BlockSpec((4096, 128), lambda i: (i, 0)),
        ]
        + [whole] * 7,
        out_specs=pl.BlockSpec((4096, 128), lambda i: (i, 0)),
        out_shape=jax.ShapeDtypeStruct((8192, 128), F32),
        scratch_shapes=[
            pltpu.VMEM((8, W, 2 * W), BF16),
            pltpu.VMEM((8, W, 2 * W), BF16),
            pltpu.VMEM((2, W, 2 * W), BF16),
            pltpu.VMEM((2, W, 2 * W), BF16),
        ],
        compiler_params=pltpu.CompilerParams(vmem_limit_bytes=48 * 1024 * 1024),
        name="update",
    )(info, mask, view, gathered, rows, *factors)


BOTH = ("row", "col")


def device(x, z, c):
    return (x * 8 + z) * 8 + c


def fan(value, axis, moves):
    total = value
    for pairs in moves:
        total = total + lax.ppermute(value, axis, pairs)
    return total


def on_device(front, pattern):
    row_place = lax.axis_index("row")
    col_place = lax.axis_index("col")
    x_place = row_place // 8
    view = front.reshape(8192, 128)
    present = pattern.reshape(2, 8)
    parity = col_place % 2
    zero = jnp.zeros((), jnp.int32)

    info = jnp.stack([present[0, 0], present[1, 0], parity])
    slab, block, *pieces = extract(info, view)

    far = lax.ppermute(block, BOTH, [(device(0, 1, 1), device(0, 0, 0))])
    below = lax.broadcasted_iota(jnp.int32, (W, W), 0)
    right = lax.broadcasted_iota(jnp.int32, (W, W), 1)
    packed = jnp.where(below >= right, block[:W], far[:W])
    extra = jnp.sum(jnp.where(below == right, far[:W], 0.0), axis=0, keepdims=True)
    packed = jnp.concatenate([packed, jnp.broadcast_to(extra, (8, W))], axis=0)
    mine = (row_place == 0) & (col_place < 2)
    diag = jnp.where(mine, jnp.where(col_place == 0, packed, block), 0.0)
    diag = fan(diag, BOTH, [
        [(device(0, 0, s), device(0, 3, s)) for s in range(2)],
        [(device(0, 0, s), device(0, 6, s)) for s in range(2)],
    ])
    diag = fan(diag, BOTH, [
        [(device(0, z, s), device(0, z + 1, s)) for z in (0, 3, 6) for s in range(2)],
        [(device(0, z, s), device(0, z - 1, s)) for z in (3, 6) for s in range(2)],
    ])
    diag = fan(diag, BOTH, [
        [(device(0, z, s), device(x, z, s)) for z in range(8) for s in range(2)]
        for x in (1, 3, 2)
    ])
    diag = fan(diag, "col", [[(s, s + y) for s in range(2)] for y in (2, 6, 4)])
    swap = [(c, c ^ 1) for c in range(8)]
    other = lax.ppermute(diag, "col", swap)
    first = jnp.where(parity == 0, diag, other)
    second = jnp.where(parity == 0, other, diag)
    factors = factor_pair(first, second)

    near = jnp.zeros((128, 128), F32)
    cross = jnp.zeros((128, 128), F32)
    offset = (row_place - col_place) % 8
    for k in range(8):
        pairs = [
            (device(x, z, s), device(x, (z + k + 4 * s) % 8, z))
            for x in range(4)
            for z in range(8)
            for s in range(2)
        ]
        got = lax.ppermute(pieces[k], BOTH, pairs)
        near = jnp.where(offset == k, got, near)
        cross = jnp.where(offset == (k + 4) % 8, got, cross)
    share = jnp.stack([near, cross])
    around = [share]
    for d in range(1, 4):
        pairs = [
            (((x + d) % 4) * 8 + z, x * 8 + z) for x in range(4) for z in range(8)
        ]
        around.append(lax.ppermute(share, "row", pairs))
    around = jnp.stack(around)
    groups = [[x * 8 + z for z in range(8)] for x in range(4)]
    gathered = lax.all_gather(around, "row", axis_index_groups=groups)

    slab = jnp.where(col_place < 2, slab, 0.0)
    slab = fan(slab, "col", [[(s, s + y) for s in range(2)] for y in (2, 6, 4)])
    twin = lax.ppermute(slab, "col", swap)
    rows = jnp.where(parity == 0, jnp.stack([slab, twin]), jnp.stack([twin, slab]))

    global_rows = jnp.arange(2, dtype=jnp.int32) * 32 + row_place
    global_cols = jnp.arange(8, dtype=jnp.int32) * 8 + col_place
    mask = jnp.where(
        (global_rows > 1)[:, None] & (global_cols > 1)[None, :], present, 0
    )
    place = jnp.stack([row_place, col_place, x_place, zero])
    out = update(place, mask, view, gathered, rows, factors)
    return out.reshape(2, 1, 256, 8, 1, 256)


def solution(mesh):
    placed = (P(None, "row", None, None, "col", None), P(None, "row", None, "col"))
    return jax.shard_map(
        on_device,
        mesh=mesh,
        in_specs=placed,
        out_specs=P(None, "row", None, None, "col", None),
        check_vma=False,
    )
```

```python
import jax
import jax.numpy as jnp
from jax import lax
from jax.experimental import pallas as pl
from jax.experimental.pallas import tpu as pltpu
from jax.sharding import PartitionSpec as P

W = 256
NB = 32
HIGHEST = lax.Precision.HIGHEST
F32 = jnp.float32
BF16 = jnp.bfloat16


def dot_nn(a, b):
    return lax.dot_general(a, b, (((1,), (0,)), ((), ())), precision=HIGHEST, preferred_element_type=F32)


def dot_nt(a, b):
    return lax.dot_general(a, b, (((1,), (1,)), ((), ())), precision=HIGHEST, preferred_element_type=F32)


def dot_tn(a, b):
    return lax.dot_general(a, b, (((0,), (0,)), ((), ())), precision=HIGHEST, preferred_element_type=F32)


def split3(x):
    hi = x.astype(BF16)
    rest = x - hi.astype(F32)
    mid = rest.astype(BF16)
    low = (rest - mid.astype(F32)).astype(BF16)
    return hi, mid, low


def eliminate(rows):
    sub = lax.broadcasted_iota(jnp.int32, (8, 384), 0)
    for t in range(4):
        x = rows[t]
        head = x[:, 0:128]
        cols = [jnp.broadcast_to(head[:, 8 * t + k : 8 * t + k + 1], (8, 128)) for k in range(8)]
        below = {
            g: [
                jnp.broadcast_to(rows[g][:, 8 * t + k : 8 * t + k + 1], (8, 128))
                for k in range(8)
            ]
            for g in range(t + 1, 4)
        }
        a = {
            (i, k): jnp.broadcast_to(cols[k][i : i + 1, :], (8, 128))
            for k in range(8)
            for i in range(k, 8)
        }
        r = [jnp.broadcast_to(x[k : k + 1, :], (8, 384)) for k in range(8)]
        for k in range(8):
            scale = lax.rsqrt(a[k, k])
            wide = jnp.concatenate([scale] * 3, axis=1)
            r[k] = r[k] * wide
            for g in below:
                below[g][k] = below[g][k] * scale
            l = {i: a[i, k] * scale for i in range(k + 1, 8)}
            for i in range(k + 1, 8):
                for j in range(k + 1, i + 1):
                    a[i, j] = a[i, j] - l[i] * l[j]
                r[i] = r[i] - jnp.concatenate([l[i]] * 3, axis=1) * r[k]
                for g in below:
                    below[g][i] = below[g][i] - l[i] * below[g][k]
        out = r[0]
        for k in range(1, 8):
            out = jnp.where(sub == k, r[k], out)
        rows[t] = out
        for g in below:
            acc = rows[g]
            for k in range(8):
                acc = acc - jnp.concatenate([below[g][k]] * 3, axis=1) * r[k]
            rows[g] = acc
    return rows


def factor_block(g_ref, u_ref, v_ref):
    lane = lax.broadcasted_iota(jnp.int32, (NB, W), 1)
    row = lax.broadcasted_iota(jnp.int32, (NB, W), 0)
    eye = (
        lax.broadcasted_iota(jnp.int32, (NB, 128), 0)
        == lax.broadcasted_iota(jnp.int32, (NB, 128), 1)
    ).astype(F32)
    tail = lax.broadcasted_iota(jnp.int32, (W - NB, W), 1)

    def panel(p, carry):
        x = jnp.concatenate([g_ref[0:NB, :], eye], axis=1)
        rows = eliminate([x[8 * t : 8 * t + 8] for t in range(4)])
        r = jnp.concatenate(rows, axis=0)
        shifted = pltpu.roll(r, 384 - NB, 1)[:, 0:W]
        at = pl.multiple_of(p * NB, NB)
        u_ref[pl.ds(at, NB), :] = jnp.where(
            lane >= row + at, pltpu.roll(r[:, 0:W], at, 1), 0.0
        )
        v_ref[pl.ds(at, NB), :] = jnp.where(
            lane <= row + at, pltpu.roll(shifted, at + NB, 1), 0.0
        )
        hi, mid, low = split3(shifted)
        left = jnp.concatenate([hi, hi, mid, mid, hi, low], axis=0)
        right = jnp.concatenate([hi, mid, hi, mid, low, hi], axis=0)
        prod = lax.dot_general(
            left, right, (((0,), (0,)), ((), ())), preferred_element_type=F32
        )
        old = pltpu.roll(g_ref[NB:W, :], W - NB, 1)
        g_ref[0 : W - NB, :] = jnp.where(tail < W - NB, old, 0.0) - prod[0 : W - NB, :]
        return carry

    lax.fori_loop(0, W // NB, panel, 0)


H = W // 2


def half_masks():
    return (
        lax.broadcasted_iota(jnp.int32, (H, H), 0),
        lax.broadcasted_iota(jnp.int32, (H, H), 1),
    )


def unpack(packed):
    below, right = half_masks()
    mixed = packed[0:H, 0:H]
    flipped = jnp.transpose(mixed)
    first = jnp.where(below >= right, mixed, flipped)
    second = jnp.where(below < right, mixed, flipped)
    second = jnp.where(below == right, packed[H : H + 1, 0:H], second)
    corner = packed[0:H, H:W]
    top = jnp.concatenate([first, jnp.transpose(corner)], axis=1)
    return jnp.concatenate([top, jnp.concatenate([corner, second], axis=1)], axis=0)


def factor_kernel(
    mine_ref, other_ref, slab_ref, twin_ref, panel_ref, row_ref, g_ref, u_ref, v0_ref, v1_ref
):
    r, c = lax.axis_index("row"), lax.axis_index("col")
    even = lax.rem(c, 2) == 0
    left = [jnp.where(even, mine_ref[i], other_ref[i]) for i in range(2)]
    right = [jnp.where(even, other_ref[i], mine_ref[i]) for i in range(2)]
    g_ref[...] = unpack(left[0])
    factor_block(g_ref, u_ref, v0_ref)
    low = jnp.concatenate(
        [jnp.transpose(left[1][0:H, 0:H]), jnp.transpose(left[1][0:H, H:W])], axis=1
    )
    a01 = jnp.concatenate([right[0][0:H], low], axis=0)
    v0 = v0_ref[...]
    pt = dot_nn(v0, a01)
    p10 = jnp.transpose(pt)
    g_ref[...] = unpack(right[1]) - dot_tn(pt, pt)
    first_u = jnp.transpose(u_ref[...])
    factor_block(g_ref, u_ref, v1_ref)
    v1 = v1_ref[...]

    raws = []
    for s in range(2):
        parts = [
            jnp.where(even == (s == 0), slab_ref[i], twin_ref[i]) for i in range(4)
        ]
        raws.append(
            jnp.concatenate(
                [jnp.concatenate(parts[2 * m : 2 * m + 2], axis=1) for m in range(2)], axis=0
            )
        )
    first = dot_nt(raws[0], v0)
    second = dot_nt(raws[1] - dot_nn(first, pt), v1)
    panel_ref[...] = jnp.where(c == 0, first, second)
    back1 = dot_nn(second, v1)
    row_ref[:, 0:W] = dot_nn(first - dot_nn(back1, p10), v0)
    row_ref[:, W : 2 * W] = back1

    @pl.when(r == 0)
    def _():
        row_ref[0:W, 0:W] = -v0
        row_ref[0:W, W : 2 * W] = jnp.zeros((W, W), F32)
        panel_ref[0:W, :] = jnp.where(c == 0, first_u, pt)

    @pl.when(r == 1)
    def _():
        row_ref[0:W, 0:W] = dot_nn(dot_nn(v1, p10), v0)
        row_ref[0:W, W : 2 * W] = -v1
        panel_ref[0:W, :] = jnp.where(c == 0, p10, jnp.transpose(u_ref[...]))


def factor_pair(mine, other, slab, twin):
    return pl.pallas_call(
        factor_kernel,
        out_shape=[
            jax.ShapeDtypeStruct((2 * W, W), F32),
            jax.ShapeDtypeStruct((2 * W, 2 * W), F32),
        ],
        scratch_shapes=[pltpu.VMEM((W, W), F32)] * 4,
        compiler_params=pltpu.CompilerParams(vmem_limit_bytes=24 * 1024 * 1024),
        name="factor_pair",
    )(mine, other, slab, twin)


def extract_kernel(pattern_ref, front_ref, slab_ref, packed_ref, *piece_refs):
    r, c = lax.axis_index("row"), lax.axis_index("col")
    parts = []
    for m in range(2):
        keep = pattern_ref[m, 0] > 0
        for h in range(2):
            part = jnp.where(keep, front_ref[m * W : m * W + W, h, :], 0.0)
            slab_ref[2 * m + h] = part
            piece_refs[2 * m + h][...] = part
            parts.append(part)
    below, right = half_masks()
    packed_ref[...] = jnp.zeros((H + 8, W), F32)

    @pl.when(r == c)
    def _():
        second = parts[1][H:W]
        diagonal = jnp.sum(jnp.where(below == right, second, 0.0), axis=0, keepdims=True)
        packed_ref[0:H, 0:H] = jnp.where(below >= right, parts[0][0:H], second)
        packed_ref[0:H, H:W] = parts[0][H:W]
        packed_ref[H : H + 8, 0:H] = jnp.broadcast_to(diagonal, (8, H))

    @pl.when(r < c)
    def _():
        packed_ref[0:H, 0:H] = parts[0][0:H]
        packed_ref[0:H, H:W] = parts[1][0:H]

    @pl.when(r > c)
    def _():
        packed_ref[0:H, 0:H] = parts[1][0:H]
        packed_ref[0:H, H:W] = parts[1][H:W]


def extract(pattern, view):
    return pl.pallas_call(
        extract_kernel,
        grid=(1,),
        in_specs=[
            pl.BlockSpec(memory_space=pltpu.SMEM),
            pl.BlockSpec((2 * W, 8, 128), lambda i: (0, 0, 0)),
        ],
        out_specs=[pl.BlockSpec(memory_space=pltpu.VMEM)] * 6,
        out_shape=[
            jax.ShapeDtypeStruct((4, W, 128), F32),
            jax.ShapeDtypeStruct((H + 8, W), F32),
        ]
        + [jax.ShapeDtypeStruct((W, 128), F32)] * 4,
        compiler_params=pltpu.CompilerParams(vmem_limit_bytes=56 * 1024 * 1024),
        name="extract",
    )(pattern, view)


FAR = ((0, 1, 7, 2), (4, 3, 5, 6))


def update_kernel(
    pattern_ref, front_hbm, q_hbm, panel_hbm, row_hbm, out_hbm,
    front_ref, q_ref, panel_ref, row_ref, out_ref, front_sem, q_sem, row_sem, out_sem,
):
    r, c = lax.axis_index("row"), lax.axis_index("col")
    x = r // 8
    q_copies, front_copies, out_copies = [], [], []

    def begin(source, target, sem):
        copy = pltpu.make_async_copy(source, target, sem)
        copy.start()
        return copy

    row_copy = begin(row_hbm, row_ref, row_sem.at[0])
    for m in range(2):
        for h in range(2):
            for s in range(2):
                i = 4 * m + 2 * h + s
                at = lax.rem(c + FAR[s][2 * m + h], 8)
                q_copies.append(begin(q_hbm.at[at], q_ref.at[i], q_sem.at[i]))
    panel_copy = begin(panel_hbm, panel_ref, row_sem.at[1])
    for m in range(2):
        half = pl.ds(m * 4096, 4096)
        front_copies.append(begin(front_hbm.at[half], front_ref.at[half], front_sem.at[m]))
        out_copies.append(
            pltpu.make_async_copy(out_ref.at[half], out_hbm.at[half], out_sem.at[m])
        )
    row_copy.wait()
    for m in range(2):
        place = r + 32 * m
        row = row_ref[m * W : m * W + W, :]
        scale, parts = [], []
        for n in range(8):
            if m == 0 and n % 4 == 0:
                for copy in q_copies[n : n + 4]:
                    copy.wait()
            j = 4 * (n // 4)
            near = lax.rem(n % 4 - x + 4, 4)
            raw = jnp.concatenate([q_ref[j + i, near] for i in (0, 2, 1, 3)], axis=1)
            prod = dot_nt(row, raw)
            keep = jnp.logical_and(
                pattern_ref[m, n] > 0, jnp.logical_and(place > 1, c + 8 * n > 1)
            )
            parts += [prod[:, 0:128], prod[:, 128:256]]
            scale.append(jnp.broadcast_to(jnp.where(keep, 1.0, 0.0), (2, 128)))
        scale = jnp.concatenate(scale, axis=0)[None]
        moved = jnp.swapaxes(jnp.stack(parts), 0, 1)
        half = pl.ds(4096 * m, 4096)
        front_copies[m].wait()
        old = front_ref[half, :].reshape(W, 16, 128)
        out_ref[half, :] = (old * scale - moved).reshape(4096, 128)
        if m == 0:
            panel_copy.wait()

        @pl.when(c < 2)
        def _():
            for h in range(2):
                out_ref[pl.ds(4096 * m + h, W, stride=16), :] = panel_ref[
                    m * W : m * W + W, 128 * h : 128 * h + 128
                ]

        out_copies[m].start()
    for copy in out_copies:
        copy.wait()


def update(pattern, view, gathered, panel, row):
    hbm = pl.BlockSpec(memory_space=pl.ANY)
    return pl.pallas_call(
        update_kernel,
        in_specs=[pl.BlockSpec(memory_space=pltpu.SMEM)] + [hbm] * 4,
        out_specs=hbm,
        out_shape=jax.ShapeDtypeStruct((8192, 128), F32),
        scratch_shapes=[
            pltpu.VMEM((8192, 128), F32),
            pltpu.VMEM((8, 4, W, 128), F32),
            pltpu.VMEM((2 * W, W), F32),
            pltpu.VMEM((2 * W, 2 * W), F32),
            pltpu.VMEM((8192, 128), F32),
            pltpu.SemaphoreType.DMA((2,)),
            pltpu.SemaphoreType.DMA((8,)),
            pltpu.SemaphoreType.DMA((2,)),
            pltpu.SemaphoreType.DMA((2,)),
        ],
        compiler_params=pltpu.CompilerParams(vmem_limit_bytes=52 * 1024 * 1024),
        name="update",
    )(pattern, view, gathered, panel, row)


BOTH = ("row", "col")


def device(x, z, c):
    return (x * 8 + z) * 8 + c


def around(value, axis, moves):
    return [lax.ppermute(value, axis, pairs) for pairs in moves]


def on_device(front, pattern):
    row_place = lax.axis_index("row")
    col_place = lax.axis_index("col")
    z_place = row_place % 8
    view = front.reshape(8192, 128)
    present = pattern.reshape(2, 8)
    slab, packed, *pieces = extract(present, front.reshape(512, 16, 128))

    at_first = (z_place == 0) | (z_place == 3) | (z_place == 6)
    at_second = (z_place == 1) | (z_place == 4) | (z_place == 7)
    steps = around(packed, BOTH, [
        [(device(0, z, s), device(0, (z + d) % 8, s)) for z in range(2) for s in range(2)]
        for d in (3, 6)
    ])
    source = (row_place < 2) & (col_place < 2)
    held = jnp.where(source, packed, 0.0) + steps[0] + steps[1]
    pieces, held = lax.optimization_barrier((pieces, held))
    plus, minus = around(held, BOTH, [
        [(device(0, z, s), device(0, (z + 1) % 8, s)) for z in (0, 3, 6, 1, 4, 7) for s in range(2)],
        [(device(0, z, s), device(0, z - 1, s)) for z in (3, 6, 4, 7) for s in range(2)],
    ])
    either = plus + minus
    diag = jnp.stack([
        jnp.where(at_first, held, jnp.where(at_second, plus, minus)),
        jnp.where(at_first, either, jnp.where(at_second, held, plus)),
    ])
    diag = jnp.where((row_place < 8) & (col_place < 2), diag, 0.0)
    share = 0.0
    for k in range(4):
        pairs = [
            (device(x, z, s), device(x, (z + FAR[s][k]) % 8, z))
            for x in range(4)
            for z in range(8)
            for s in range(2)
        ]
        share = share + lax.ppermute(pieces[k], BOTH, pairs)
    line = [share]
    for d in range(1, 4):
        pairs = [
            (((x + d) % 4) * 8 + z, x * 8 + z) for x in range(4) for z in range(8)
        ]
        line.append(lax.ppermute(share, "row", pairs))
    line = jnp.stack(line)
    line, diag = lax.optimization_barrier((line, diag))
    groups = [[x * 8 + z for z in range(8)] for x in range(4)]
    gathered = lax.all_gather(line, "row", axis_index_groups=groups)

    steps = around(diag, BOTH, [
        [(device(0, z, s), device(x, z, s)) for z in range(8) for s in range(2)]
        for x in (1, 3, 2)
    ])
    diag = diag + steps[0] + steps[1] + steps[2]
    fan_y = [[(s, s + y) for s in range(2)] for y in (2, 6, 4)]
    steps = around(slab, "col", fan_y)
    slab = jnp.where(col_place < 2, slab, steps[0] + steps[1] + steps[2])
    slab, diag = lax.optimization_barrier((slab, diag))
    steps = around(diag, "col", fan_y)
    diag = diag + steps[0] + steps[1] + steps[2]
    swap = [(c, c ^ 1) for c in range(8)]
    other = lax.ppermute(diag, "col", swap)

    twin = lax.ppermute(slab, "col", swap)

    panel, row = factor_pair(diag, other, slab, twin)
    out = update(present, view, gathered, panel, row)
    return out.reshape(2, 1, 256, 8, 1, 256)


def solution(mesh):
    placed = (P(None, "row", None, None, "col", None), P(None, "row", None, "col"))
    return jax.shard_map(
        on_device,
        mesh=mesh,
        in_specs=placed,
        out_specs=P(None, "row", None, None, "col", None),
        check_vma=False,
    )
```

```python
import jax
import jax.numpy as jnp
from jax import lax
from jax.experimental import pallas as pl
from jax.experimental.pallas import tpu as pltpu
from jax.sharding import PartitionSpec as P

W = 256
NB = 32
HIGHEST = lax.Precision.HIGHEST
F32 = jnp.float32
BF16 = jnp.bfloat16


def dot_nn(a, b):
    return lax.dot_general(a, b, (((1,), (0,)), ((), ())), precision=HIGHEST, preferred_element_type=F32)


def dot_nt(a, b):
    return lax.dot_general(a, b, (((1,), (1,)), ((), ())), precision=HIGHEST, preferred_element_type=F32)


def dot_tn(a, b):
    return lax.dot_general(a, b, (((0,), (0,)), ((), ())), precision=HIGHEST, preferred_element_type=F32)


def split3(x):
    hi = x.astype(BF16)
    rest = x - hi.astype(F32)
    mid = rest.astype(BF16)
    low = (rest - mid.astype(F32)).astype(BF16)
    return hi, mid, low


def eliminate(rows):
    sub = lax.broadcasted_iota(jnp.int32, (8, 384), 0)
    for t in range(4):
        x = rows[t]
        head = x[:, 0:128]
        cols = [jnp.broadcast_to(head[:, 8 * t + k : 8 * t + k + 1], (8, 128)) for k in range(8)]
        below = {
            g: [
                jnp.broadcast_to(rows[g][:, 8 * t + k : 8 * t + k + 1], (8, 128))
                for k in range(8)
            ]
            for g in range(t + 1, 4)
        }
        a = {
            (i, k): jnp.broadcast_to(cols[k][i : i + 1, :], (8, 128))
            for k in range(8)
            for i in range(k, 8)
        }
        r = [jnp.broadcast_to(x[k : k + 1, :], (8, 384)) for k in range(8)]
        for k in range(8):
            scale = lax.rsqrt(a[k, k])
            wide = jnp.concatenate([scale] * 3, axis=1)
            r[k] = r[k] * wide
            for g in below:
                below[g][k] = below[g][k] * scale
            l = {i: a[i, k] * scale for i in range(k + 1, 8)}
            for i in range(k + 1, 8):
                for j in range(k + 1, i + 1):
                    a[i, j] = a[i, j] - l[i] * l[j]
                r[i] = r[i] - jnp.concatenate([l[i]] * 3, axis=1) * r[k]
                for g in below:
                    below[g][i] = below[g][i] - l[i] * below[g][k]
        out = r[0]
        for k in range(1, 8):
            out = jnp.where(sub == k, r[k], out)
        rows[t] = out
        for g in below:
            acc = rows[g]
            for k in range(8):
                acc = acc - jnp.concatenate([below[g][k]] * 3, axis=1) * r[k]
            rows[g] = acc
    return rows


def factor_block(g_ref, u_ref, v_ref, beside=None):
    lane = lax.broadcasted_iota(jnp.int32, (NB, W), 1)
    row = lax.broadcasted_iota(jnp.int32, (NB, W), 0)
    eye = (
        lax.broadcasted_iota(jnp.int32, (NB, 128), 0)
        == lax.broadcasted_iota(jnp.int32, (NB, 128), 1)
    ).astype(F32)
    tail = lax.broadcasted_iota(jnp.int32, (W - NB, W), 1)

    def panel(p, carry):
        if beside is not None:
            beside(p)
        x = jnp.concatenate([g_ref[0:NB, :], eye], axis=1)
        rows = eliminate([x[8 * t : 8 * t + 8] for t in range(4)])
        r = jnp.concatenate(rows, axis=0)
        shifted = pltpu.roll(r, 384 - NB, 1)[:, 0:W]
        at = pl.multiple_of(p * NB, NB)
        u_ref[pl.ds(at, NB), :] = jnp.where(
            lane >= row + at, pltpu.roll(r[:, 0:W], at, 1), 0.0
        )
        v_ref[pl.ds(at, NB), :] = jnp.where(
            lane <= row + at, pltpu.roll(shifted, at + NB, 1), 0.0
        )
        hi, mid, low = split3(shifted)
        left = jnp.concatenate([hi, hi, mid, mid, hi, low], axis=0)
        right = jnp.concatenate([hi, mid, hi, mid, low, hi], axis=0)
        prod = lax.dot_general(
            left, right, (((0,), (0,)), ((), ())), preferred_element_type=F32
        )
        old = pltpu.roll(g_ref[NB:W, :], W - NB, 1)
        g_ref[0 : W - NB, :] = jnp.where(tail < W - NB, old, 0.0) - prod[0 : W - NB, :]
        return carry

    lax.fori_loop(0, W // NB, panel, 0)


H = W // 2
PACKED = H + 16
PIECE = PACKED // 2


def half_masks():
    return (
        lax.broadcasted_iota(jnp.int32, (H, H), 0),
        lax.broadcasted_iota(jnp.int32, (H, H), 1),
    )


def unpack(packed):
    below, right = half_masks()
    mixed = packed[0:H, 0:H]
    flipped = jnp.transpose(mixed)
    first = jnp.where(below >= right, mixed, flipped)
    second = jnp.where(below < right, mixed, flipped)
    second = jnp.where(below == right, packed[H : H + 1, 0:H], second)
    corner = packed[0:H, H:W]
    top = jnp.concatenate([first, jnp.transpose(corner)], axis=1)
    return jnp.concatenate([top, jnp.concatenate([corner, second], axis=1)], axis=0)


def factor_kernel(
    mine_ref, other_ref, slab_ref, twin_ref,
    panel_ref, row_ref, g_ref, u_ref, v0_ref, v1_ref, r0_ref, r1_ref,
):
    r, c = lax.axis_index("row"), lax.axis_index("col")
    even = lax.rem(c, 2) == 0

    def joined(t, side):
        spots = [lax.rem(x - r // 8 + 4, 4) for x in range(4)]
        tall = [
            jnp.where(even == side, mine_ref[spot, t], other_ref[spot, t]) for spot in spots
        ]
        return jnp.concatenate(
            [jnp.concatenate(tall[2 * h : 2 * h + 2], axis=0) for h in range(2)], axis=1
        )

    g_ref[...] = unpack(joined(0, True))
    factor_block(g_ref, u_ref, v0_ref)
    upper, lower = joined(0, False), joined(1, True)
    low = jnp.concatenate(
        [jnp.transpose(lower[0:H, 0:H]), jnp.transpose(lower[0:H, H:W])], axis=1
    )
    a01 = jnp.concatenate([upper[0:H], low], axis=0)
    v0 = v0_ref[...]
    pt = dot_nn(v0, a01)
    p10 = jnp.transpose(pt)
    g_ref[...] = unpack(joined(1, False)) - dot_tn(pt, pt)
    first_u = jnp.transpose(u_ref[...])
    for s, ref in enumerate((r0_ref, r1_ref)):
        for m in range(2):
            for h in range(2):
                i = 2 * m + h
                ref[m * W : m * W + W, h * H : h * H + H] = jnp.where(
                    even == (s == 0), slab_ref[i], twin_ref[i]
                )

    def beside(p):
        span = pl.ds(pl.multiple_of(p * 64, 64), 64)
        first = dot_nt(r0_ref[span, :], v0_ref[...])
        panel_ref[span, :] = first
        r1_ref[span, :] = r1_ref[span, :] - dot_nn(first, pt)
        r0_ref[span, :] = dot_nn(first, v0_ref[...])

    factor_block(g_ref, u_ref, v1_ref, beside)
    v1 = v1_ref[...]
    p10v0 = dot_nn(p10, v0)
    second = dot_nt(r1_ref[...], v1)
    back1 = dot_nn(second, v1)
    row_ref[:, 0:W] = r0_ref[...] - dot_nn(back1, p10v0)
    row_ref[:, W : 2 * W] = back1

    @pl.when(c != 0)
    def _():
        panel_ref[...] = second

    @pl.when(r == 0)
    def _():
        row_ref[0:W, 0:W] = -v0
        row_ref[0:W, W : 2 * W] = jnp.zeros((W, W), F32)
        panel_ref[0:W, :] = jnp.where(c == 0, first_u, pt)

    @pl.when(r == 1)
    def _():
        row_ref[0:W, 0:W] = dot_nn(v1, p10v0)
        row_ref[0:W, W : 2 * W] = -v1
        panel_ref[0:W, :] = jnp.where(c == 0, p10, jnp.transpose(u_ref[...]))


def factor_pair(mine, other, slab, twin):
    return pl.pallas_call(
        factor_kernel,
        out_shape=[
            jax.ShapeDtypeStruct((2 * W, W), F32),
            jax.ShapeDtypeStruct((2 * W, 2 * W), F32),
        ],
        scratch_shapes=[pltpu.VMEM((W, W), F32)] * 4
        + [pltpu.VMEM((2 * W, W), F32)] * 2,
        compiler_params=pltpu.CompilerParams(vmem_limit_bytes=24 * 1024 * 1024),
        name="factor_pair",
    )(mine, other, slab, twin)


def extract_kernel(pattern_ref, front_ref, slab_ref, packed_ref, *piece_refs):
    r, c = lax.axis_index("row"), lax.axis_index("col")
    parts = []
    for m in range(2):
        keep = pattern_ref[m, 0] > 0
        for h in range(2):
            part = jnp.where(keep, front_ref[m * W : m * W + W, h, :], 0.0)
            slab_ref[2 * m + h] = part
            piece_refs[2 * m + h][...] = part
            parts.append(part)
    below, right = half_masks()

    def put(first, second, extra):
        packed_ref[...] = jnp.concatenate(
            [first, jnp.broadcast_to(extra, (PACKED - H, H)), second, jnp.zeros((PACKED - H, H), F32)],
            axis=0,
        )

    @pl.when(r == c)
    def _():
        second = parts[1][H:W]
        diagonal = jnp.sum(jnp.where(below == right, second, 0.0), axis=0, keepdims=True)
        put(jnp.where(below >= right, parts[0][0:H], second), parts[0][H:W], diagonal)

    zero = jnp.zeros((1, H), F32)

    @pl.when(r < c)
    def _():
        put(parts[0][0:H], parts[1][0:H], zero)

    @pl.when(r > c)
    def _():
        put(parts[1][0:H], parts[1][H:W], zero)


def extract(pattern, view):
    return pl.pallas_call(
        extract_kernel,
        grid=(1,),
        in_specs=[
            pl.BlockSpec(memory_space=pltpu.SMEM),
            pl.BlockSpec((2 * W, 8, 128), lambda i: (0, 0, 0)),
        ],
        out_specs=[pl.BlockSpec(memory_space=pltpu.VMEM)] * 6,
        out_shape=[
            jax.ShapeDtypeStruct((4, W, 128), F32),
            jax.ShapeDtypeStruct((2 * PACKED, H), F32),
        ]
        + [jax.ShapeDtypeStruct((W, 128), F32)] * 4,
        compiler_params=pltpu.CompilerParams(vmem_limit_bytes=56 * 1024 * 1024),
        name="extract",
    )(pattern, view)


FAR = ((0, 1, 7, 2), (4, 3, 5, 6))


def update_kernel(
    pattern_ref, front_hbm, q_hbm, panel_ref, row_ref, out_hbm,
    front_ref, q_ref, out_ref, front_sem, q_sem, out_sem,
):
    r, c = lax.axis_index("row"), lax.axis_index("col")
    x = r // 8
    q_copies, front_copies, out_copies = [], [], []

    def begin(source, target, sem):
        copy = pltpu.make_async_copy(source, target, sem)
        copy.start()
        return copy

    for m in range(2):
        for h in range(2):
            for s in range(2):
                i = 4 * m + 2 * h + s
                at = lax.rem(c + FAR[s][2 * m + h], 8)
                q_copies.append(begin(q_hbm.at[at], q_ref.at[i], q_sem.at[i]))
    for m in range(2):
        half = pl.ds(m * 4096, 4096)
        front_copies.append(begin(front_hbm.at[half], front_ref.at[half], front_sem.at[m]))
        out_copies.append(
            pltpu.make_async_copy(out_ref.at[half], out_hbm.at[half], out_sem.at[m])
        )
    for m in range(2):
        place = r + 32 * m
        row = row_ref[m * W : m * W + W, :]
        scale, parts = [], []
        for n in range(8):
            if m == 0 and n % 4 == 0:
                for copy in q_copies[n : n + 4]:
                    copy.wait()
            j = 4 * (n // 4)
            near = lax.rem(n % 4 - x + 4, 4)
            raw = jnp.concatenate([q_ref[j + i, near] for i in (0, 2, 1, 3)], axis=1)
            prod = dot_nt(row, raw)
            keep = jnp.logical_and(
                pattern_ref[m, n] > 0, jnp.logical_and(place > 1, c + 8 * n > 1)
            )
            parts += [prod[:, 0:128], prod[:, 128:256]]
            scale.append(jnp.broadcast_to(jnp.where(keep, 1.0, 0.0), (2, 128)))
        scale = jnp.concatenate(scale, axis=0)[None]
        moved = jnp.swapaxes(jnp.stack(parts), 0, 1)
        half = pl.ds(4096 * m, 4096)
        front_copies[m].wait()
        old = front_ref[half, :].reshape(W, 16, 128)
        out_ref[half, :] = (old * scale - moved).reshape(4096, 128)

        @pl.when(c < 2)
        def _():
            for h in range(2):
                out_ref[pl.ds(4096 * m + h, W, stride=16), :] = panel_ref[
                    m * W : m * W + W, 128 * h : 128 * h + 128
                ]

        out_copies[m].start()
    for copy in out_copies:
        copy.wait()


def update(pattern, view, gathered, panel, row):
    hbm = pl.BlockSpec(memory_space=pl.ANY)
    vmem = pl.BlockSpec(memory_space=pltpu.VMEM)
    return pl.pallas_call(
        update_kernel,
        in_specs=[pl.BlockSpec(memory_space=pltpu.SMEM), hbm, hbm, vmem, vmem],
        out_specs=hbm,
        out_shape=jax.ShapeDtypeStruct((8192, 128), F32),
        scratch_shapes=[
            pltpu.VMEM((8192, 128), F32),
            pltpu.VMEM((8, 4, W, 128), F32),
            pltpu.VMEM((8192, 128), F32),
            pltpu.SemaphoreType.DMA((2,)),
            pltpu.SemaphoreType.DMA((8,)),
            pltpu.SemaphoreType.DMA((2,)),
        ],
        compiler_params=pltpu.CompilerParams(vmem_limit_bytes=52 * 1024 * 1024),
        name="update",
    )(pattern, view, gathered, panel, row)


BOTH = ("row", "col")


def device(x, z, c):
    return (x * 8 + z) * 8 + c


def around(value, axis, moves):
    return [lax.ppermute(value, axis, pairs) for pairs in moves]


def on_device(front, pattern):
    row_place = lax.axis_index("row")
    col_place = lax.axis_index("col")
    view = front.reshape(8192, 128)
    present = pattern.reshape(2, 8)
    slab, packed, *pieces = extract(present, front.reshape(512, 16, 128))

    x_moves = [
        [(((x + d) % 4) * 8 + z, x * 8 + z) for x in range(4) for z in range(8)]
        for d in (1, 2, 3)
    ]
    swap = [(c, c ^ 1) for c in range(8)]
    groups = [[x * 8 + z for z in range(8)] for x in range(4)]
    z_place = row_place % 8

    across = lax.all_gather(packed, "col")
    held = jnp.where(col_place % 2 == 0, across[0], across[1])

    share = 0.0
    for k in range(4):
        pairs = [
            (device(x, z, s), device(x, (z + FAR[s][k]) % 8, z))
            for x in range(4)
            for z in range(8)
            for s in range(2)
        ]
        share = share + lax.ppermute(pieces[k], BOTH, pairs)
    line = jnp.stack([share] + around(share, "row", x_moves))
    slab = jnp.where(col_place < 2, slab, lax.ppermute(slab, "col", [(0, 4), (1, 5)]))
    line, held, slab = lax.optimization_barrier((line, held, slab))
    gathered = lax.all_gather(line, "row", axis_index_groups=groups)

    quarters = [held[PIECE * x : PIECE * x + PIECE] for x in range(4)]
    held = jnp.where(row_place < 2, quarters[0], 0.0)
    for x in (1, 3, 2):
        held = held + lax.ppermute(quarters[x], "row", [(z, x * 8 + z) for z in range(2)])
    moved = lax.ppermute(slab, "col", [(0, 2), (1, 3), (4, 6), (5, 7)])

    at_first = (z_place == 0) | (z_place == 3) | (z_place == 6)
    at_second = (z_place == 1) | (z_place == 4) | (z_place == 7)
    steps = around(held, "row", [
        [(x * 8 + z, x * 8 + (z + d) % 8) for x in range(4) for z in range(2)]
        for d in (3, 6)
    ])
    held = held + steps[0] + steps[1]
    plus, minus = around(held, "row", [
        [(x * 8 + z, x * 8 + (z + 1) % 8) for x in range(4) for z in (0, 3, 6, 1, 4, 7)],
        [(x * 8 + z, x * 8 + z - 1) for x in range(4) for z in (3, 6, 4, 7)],
    ])
    either = plus + minus
    diag = jnp.stack([
        jnp.where(at_first, held, jnp.where(at_second, plus, minus)),
        jnp.where(at_first, either, jnp.where(at_second, held, plus)),
    ])
    slab = jnp.where(col_place % 4 < 2, slab, moved)
    diag, slab = lax.optimization_barrier((diag, slab))
    twin = lax.ppermute(slab, "col", swap)
    mine = jnp.stack([diag] + around(diag, "row", x_moves))
    other = lax.ppermute(mine, "col", swap)

    panel, row = factor_pair(mine, other, slab, twin)
    out = update(present, view, gathered, panel, row)
    return out.reshape(2, 1, 256, 8, 1, 256)


def solution(mesh):
    placed = (P(None, "row", None, None, "col", None), P(None, "row", None, "col"))
    return jax.shard_map(
        on_device,
        mesh=mesh,
        in_specs=placed,
        out_specs=P(None, "row", None, None, "col", None),
        check_vma=False,
    )
```

```python
import jax
import jax.numpy as jnp
from jax import lax
from jax.experimental import pallas as pl
from jax.experimental.pallas import tpu as pltpu
from jax.sharding import PartitionSpec as P

W = 256
NB = 32
HIGHEST = lax.Precision.HIGHEST
F32 = jnp.float32
BF16 = jnp.bfloat16


def dot_nn(a, b):
    return lax.dot_general(a, b, (((1,), (0,)), ((), ())), precision=HIGHEST, preferred_element_type=F32)


def dot_nt(a, b):
    return lax.dot_general(a, b, (((1,), (1,)), ((), ())), precision=HIGHEST, preferred_element_type=F32)


def dot_tn(a, b):
    return lax.dot_general(a, b, (((0,), (0,)), ((), ())), precision=HIGHEST, preferred_element_type=F32)


def split3(x):
    hi = x.astype(BF16)
    rest = x - hi.astype(F32)
    mid = rest.astype(BF16)
    low = (rest - mid.astype(F32)).astype(BF16)
    return hi, mid, low


def eliminate(rows):
    sub = lax.broadcasted_iota(jnp.int32, (8, 384), 0)
    for t in range(4):
        x = rows[t]
        head = x[:, 0:128]
        cols = [jnp.broadcast_to(head[:, 8 * t + k : 8 * t + k + 1], (8, 128)) for k in range(8)]
        below = {
            g: [
                jnp.broadcast_to(rows[g][:, 8 * t + k : 8 * t + k + 1], (8, 128))
                for k in range(8)
            ]
            for g in range(t + 1, 4)
        }
        a = {
            (i, k): jnp.broadcast_to(cols[k][i : i + 1, :], (8, 128))
            for k in range(8)
            for i in range(k, 8)
        }
        r = [jnp.broadcast_to(x[k : k + 1, :], (8, 384)) for k in range(8)]
        for k in range(8):
            scale = lax.rsqrt(a[k, k])
            wide = jnp.concatenate([scale] * 3, axis=1)
            r[k] = r[k] * wide
            for g in below:
                below[g][k] = below[g][k] * scale
            l = {i: a[i, k] * scale for i in range(k + 1, 8)}
            for i in range(k + 1, 8):
                for j in range(k + 1, i + 1):
                    a[i, j] = a[i, j] - l[i] * l[j]
                r[i] = r[i] - jnp.concatenate([l[i]] * 3, axis=1) * r[k]
                for g in below:
                    below[g][i] = below[g][i] - l[i] * below[g][k]
        out = r[0]
        for k in range(1, 8):
            out = jnp.where(sub == k, r[k], out)
        rows[t] = out
        for g in below:
            acc = rows[g]
            for k in range(8):
                acc = acc - jnp.concatenate([below[g][k]] * 3, axis=1) * r[k]
            rows[g] = acc
    return rows


def factor_block(g_ref, u_ref, v_ref, beside=None):
    lane = lax.broadcasted_iota(jnp.int32, (NB, W), 1)
    row = lax.broadcasted_iota(jnp.int32, (NB, W), 0)
    eye = (
        lax.broadcasted_iota(jnp.int32, (NB, 128), 0)
        == lax.broadcasted_iota(jnp.int32, (NB, 128), 1)
    ).astype(F32)
    tail = lax.broadcasted_iota(jnp.int32, (W - NB, W), 1)

    def panel(p, carry):
        if beside is not None:
            beside(p)
        x = jnp.concatenate([g_ref[0:NB, :], eye], axis=1)
        rows = eliminate([x[8 * t : 8 * t + 8] for t in range(4)])
        r = jnp.concatenate(rows, axis=0)
        shifted = pltpu.roll(r, 384 - NB, 1)[:, 0:W]
        at = pl.multiple_of(p * NB, NB)
        u_ref[pl.ds(at, NB), :] = jnp.where(
            lane >= row + at, pltpu.roll(r[:, 0:W], at, 1), 0.0
        )
        v_ref[pl.ds(at, NB), :] = jnp.where(
            lane <= row + at, pltpu.roll(shifted, at + NB, 1), 0.0
        )
        hi, mid, low = split3(shifted)
        left = jnp.concatenate([hi, hi, mid, mid, hi, low], axis=0)
        right = jnp.concatenate([hi, mid, hi, mid, low, hi], axis=0)
        prod = lax.dot_general(
            left, right, (((0,), (0,)), ((), ())), preferred_element_type=F32
        )
        old = pltpu.roll(g_ref[NB:W, :], W - NB, 1)
        g_ref[0 : W - NB, :] = jnp.where(tail < W - NB, old, 0.0) - prod[0 : W - NB, :]
        return carry

    lax.fori_loop(0, W // NB, panel, 0)


H = W // 2
PACKED = H + 16
PIECE = PACKED // 2


def half_masks():
    return (
        lax.broadcasted_iota(jnp.int32, (H, H), 0),
        lax.broadcasted_iota(jnp.int32, (H, H), 1),
    )


def unpack(packed):
    below, right = half_masks()
    mixed = packed[0:H, 0:H]
    flipped = jnp.transpose(mixed)
    first = jnp.where(below >= right, mixed, flipped)
    second = jnp.where(below < right, mixed, flipped)
    second = jnp.where(below == right, packed[H : H + 1, 0:H], second)
    corner = packed[0:H, H:W]
    top = jnp.concatenate([first, jnp.transpose(corner)], axis=1)
    return jnp.concatenate([top, jnp.concatenate([corner, second], axis=1)], axis=0)


def factor_kernel(
    mine_ref, other_ref, slab_ref, twin_ref,
    panel_ref, row_ref, g_ref, u_ref, v0_ref, v1_ref, r0_ref, r1_ref,
):
    r, c = lax.axis_index("row"), lax.axis_index("col")
    even = lax.rem(c, 2) == 0

    def joined(t, side):
        spots = [lax.rem(x - r // 8 + 4, 4) for x in range(4)]
        tall = [
            jnp.where(even == side, mine_ref[spot, t], other_ref[spot, t]) for spot in spots
        ]
        return jnp.concatenate(
            [jnp.concatenate(tall[2 * h : 2 * h + 2], axis=0) for h in range(2)], axis=1
        )

    g_ref[...] = unpack(joined(0, True))
    factor_block(g_ref, u_ref, v0_ref)
    upper, lower = joined(0, False), joined(1, True)
    low = jnp.concatenate(
        [jnp.transpose(lower[0:H, 0:H]), jnp.transpose(lower[0:H, H:W])], axis=1
    )
    a01 = jnp.concatenate([upper[0:H], low], axis=0)
    v0 = v0_ref[...]
    pt = dot_nn(v0, a01)
    g_ref[...] = unpack(joined(1, False)) - dot_tn(pt, pt)
    first_u = jnp.transpose(u_ref[...])
    for s, ref in enumerate((r0_ref, r1_ref)):
        for m in range(2):
            for h in range(2):
                i = 2 * m + h
                ref[m * W : m * W + W, h * H : h * H + H] = jnp.where(
                    even == (s == 0), slab_ref[i], twin_ref[i]
                )

    def beside(p):
        span = pl.ds(pl.multiple_of(p * 64, 64), 64)
        first = dot_nt(r0_ref[span, :], v0_ref[...])
        panel_ref[span, :] = first
        r1_ref[span, :] = r1_ref[span, :] - dot_nn(first, pt)
        r0_ref[span, :] = dot_nn(first, v0_ref[...])

    factor_block(g_ref, u_ref, v1_ref, beside)
    v1 = v1_ref[...]
    p10v0 = dot_tn(pt, v0)
    second = dot_nt(r1_ref[...], v1)
    back1 = dot_nn(second, v1)
    row_ref[:, 0:W] = r0_ref[...] - dot_nn(back1, p10v0)
    row_ref[:, W : 2 * W] = back1

    @pl.when(c != 0)
    def _():
        panel_ref[...] = second

    @pl.when(r == 0)
    def _():
        row_ref[0:W, 0:W] = -v0
        row_ref[0:W, W : 2 * W] = jnp.zeros((W, W), F32)
        panel_ref[0:W, :] = jnp.where(c == 0, first_u, pt)

    @pl.when(r == 1)
    def _():
        row_ref[0:W, 0:W] = dot_nn(v1, p10v0)
        row_ref[0:W, W : 2 * W] = -v1
        panel_ref[0:W, :] = jnp.transpose(jnp.where(c == 0, pt, u_ref[...]))


def factor_pair(mine, other, slab, twin):
    return pl.pallas_call(
        factor_kernel,
        out_shape=[
            jax.ShapeDtypeStruct((2 * W, W), F32),
            jax.ShapeDtypeStruct((2 * W, 2 * W), F32),
        ],
        scratch_shapes=[pltpu.VMEM((W, W), F32)] * 4
        + [pltpu.VMEM((2 * W, W), F32)] * 2,
        compiler_params=pltpu.CompilerParams(vmem_limit_bytes=24 * 1024 * 1024),
        name="factor_pair",
    )(mine, other, slab, twin)


def extract_kernel(pattern_ref, front_ref, slab_ref, packed_ref, *piece_refs):
    r, c = lax.axis_index("row"), lax.axis_index("col")
    parts = []
    for m in range(2):
        keep = pattern_ref[m, 0] > 0
        for h in range(2):
            part = jnp.where(keep, front_ref[m * W : m * W + W, h, :], 0.0)
            slab_ref[2 * m + h] = part
            piece_refs[2 * m + h][...] = part
            parts.append(part)
    below, right = half_masks()

    def put(first, second, extra):
        packed_ref[...] = jnp.concatenate(
            [first, jnp.broadcast_to(extra, (PACKED - H, H)), second, jnp.zeros((PACKED - H, H), F32)],
            axis=0,
        )

    @pl.when(r == c)
    def _():
        second = parts[1][H:W]
        diagonal = jnp.sum(jnp.where(below == right, second, 0.0), axis=0, keepdims=True)
        put(jnp.where(below >= right, parts[0][0:H], second), parts[0][H:W], diagonal)

    zero = jnp.zeros((1, H), F32)

    @pl.when(r < c)
    def _():
        put(parts[0][0:H], parts[1][0:H], zero)

    @pl.when(r > c)
    def _():
        put(parts[1][0:H], parts[1][H:W], zero)


def extract(pattern, view):
    return pl.pallas_call(
        extract_kernel,
        grid=(1,),
        in_specs=[
            pl.BlockSpec(memory_space=pltpu.SMEM),
            pl.BlockSpec((2 * W, 8, 128), lambda i: (0, 0, 0)),
        ],
        out_specs=[pl.BlockSpec(memory_space=pltpu.VMEM)] * 6,
        out_shape=[
            jax.ShapeDtypeStruct((4, W, 128), F32),
            jax.ShapeDtypeStruct((2 * PACKED, H), F32),
        ]
        + [jax.ShapeDtypeStruct((W, 128), F32)] * 4,
        compiler_params=pltpu.CompilerParams(vmem_limit_bytes=56 * 1024 * 1024),
        name="extract",
    )(pattern, view)


FAR = ((0, 1, 7, 2), (4, 3, 5, 6))


def update_kernel(
    pattern_ref, front_hbm, q_hbm, panel_ref, row_ref, out_hbm,
    front_ref, q_ref, out_ref, front_sem, q_sem, out_sem,
):
    r, c = lax.axis_index("row"), lax.axis_index("col")
    x = r // 8
    q_copies, front_copies, out_copies = [], [], []

    def begin(source, target, sem):
        copy = pltpu.make_async_copy(source, target, sem)
        copy.start()
        return copy

    for m in range(2):
        for h in range(2):
            for s in range(2):
                i = 4 * m + 2 * h + s
                at = lax.rem(c + FAR[s][2 * m + h], 8)
                q_copies.append(begin(q_hbm.at[at], q_ref.at[i], q_sem.at[i]))
    for m in range(2):
        half = pl.ds(m * 4096, 4096)
        front_copies.append(begin(front_hbm.at[half], front_ref.at[half], front_sem.at[m]))
        out_copies.append(
            pltpu.make_async_copy(out_ref.at[half], out_hbm.at[half], out_sem.at[m])
        )
    for m in range(2):
        place = r + 32 * m
        row = row_ref[m * W : m * W + W, :]
        scale, parts = [], []
        for n in range(8):
            if m == 0 and n % 4 == 0:
                for copy in q_copies[n : n + 4]:
                    copy.wait()
            j = 4 * (n // 4)
            near = lax.rem(n % 4 - x + 4, 4)
            raw = jnp.concatenate([q_ref[j + i, near] for i in (0, 2, 1, 3)], axis=1)
            prod = dot_nt(row, raw)
            keep = jnp.logical_and(
                pattern_ref[m, n] > 0, jnp.logical_and(place > 1, c + 8 * n > 1)
            )
            parts += [prod[:, 0:128], prod[:, 128:256]]
            scale.append(jnp.broadcast_to(jnp.where(keep, 1.0, 0.0), (2, 128)))
        scale = jnp.concatenate(scale, axis=0)[None]
        moved = jnp.swapaxes(jnp.stack(parts), 0, 1)
        half = pl.ds(4096 * m, 4096)
        front_copies[m].wait()
        old = front_ref[half, :].reshape(W, 16, 128)
        out_ref[half, :] = (old * scale - moved).reshape(4096, 128)

        @pl.when(c < 2)
        def _():
            for h in range(2):
                out_ref[pl.ds(4096 * m + h, W, stride=16), :] = panel_ref[
                    m * W : m * W + W, 128 * h : 128 * h + 128
                ]

        out_copies[m].start()
    for copy in out_copies:
        copy.wait()


def update(pattern, view, gathered, panel, row):
    hbm = pl.BlockSpec(memory_space=pl.ANY)
    vmem = pl.BlockSpec(memory_space=pltpu.VMEM)
    return pl.pallas_call(
        update_kernel,
        in_specs=[pl.BlockSpec(memory_space=pltpu.SMEM), hbm, hbm, vmem, vmem],
        out_specs=hbm,
        out_shape=jax.ShapeDtypeStruct((8192, 128), F32),
        scratch_shapes=[
            pltpu.VMEM((8192, 128), F32),
            pltpu.VMEM((8, 4, W, 128), F32),
            pltpu.VMEM((8192, 128), F32),
            pltpu.SemaphoreType.DMA((2,)),
            pltpu.SemaphoreType.DMA((8,)),
            pltpu.SemaphoreType.DMA((2,)),
        ],
        compiler_params=pltpu.CompilerParams(vmem_limit_bytes=52 * 1024 * 1024),
        name="update",
    )(pattern, view, gathered, panel, row)


BOTH = ("row", "col")


def device(x, z, c):
    return (x * 8 + z) * 8 + c


def around(value, axis, moves):
    return [lax.ppermute(value, axis, pairs) for pairs in moves]


def on_device(front, pattern):
    row_place = lax.axis_index("row")
    col_place = lax.axis_index("col")
    view = front.reshape(8192, 128)
    present = pattern.reshape(2, 8)
    slab, packed, *pieces = extract(present, front.reshape(512, 16, 128))

    x_moves = [
        [(((x + d) % 4) * 8 + z, x * 8 + z) for x in range(4) for z in range(8)]
        for d in (1, 2, 3)
    ]
    swap = [(c, c ^ 1) for c in range(8)]
    groups = [[x * 8 + z for z in range(8)] for x in range(4)]

    across = lax.all_gather(packed, "col")
    held = jnp.where(col_place % 2 == 0, across[0], across[1])

    share = 0.0
    for k in range(4):
        pairs = [
            (device(x, z, s), device(x, (z + FAR[s][k]) % 8, z))
            for x in range(4)
            for z in range(8)
            for s in range(2)
        ]
        share = share + lax.ppermute(pieces[k], BOTH, pairs)
    line = jnp.stack([share] + around(share, "row", x_moves))
    moved = lax.ppermute(slab, "col", [(0, 4), (1, 5)])
    line, moved = lax.optimization_barrier((line, moved))
    gathered = lax.all_gather(line, "row", axis_index_groups=groups)
    slab = jnp.where(col_place < 2, slab, moved)

    quarters = [held[PIECE * x : PIECE * x + PIECE] for x in range(4)]
    held = jnp.where(row_place < 2, quarters[0], 0.0)
    for x in (1, 3, 2):
        held = held + lax.ppermute(quarters[x], "row", [(z, x * 8 + z) for z in range(2)])
    start = held
    moved = lax.ppermute(slab, "col", [(0, 2), (1, 3), (4, 6), (5, 7)])

    for d in (2, 6, 4):
        held = held + lax.ppermute(start, "row", [
            (x * 8 + z, x * 8 + (z + d) % 8) for x in range(4) for z in range(2)
        ])
    after = lax.ppermute(held, "row", [
        (x * 8 + z, x * 8 + (z + 1) % 8) for x in range(4) for z in range(8)
    ])
    even = row_place % 2 == 0
    diag = jnp.stack([jnp.where(even, held, after), jnp.where(even, after, held)])
    slab = jnp.where(col_place % 4 < 2, slab, moved)
    diag, slab = lax.optimization_barrier((diag, slab))
    twin = lax.ppermute(slab, "col", swap)
    mine = jnp.stack([diag] + around(diag, "row", x_moves))
    other = lax.ppermute(mine, "col", swap)

    panel, row = factor_pair(mine, other, slab, twin)
    out = update(present, view, gathered, panel, row)
    return out.reshape(2, 1, 256, 8, 1, 256)


def solution(mesh):
    placed = (P(None, "row", None, None, "col", None), P(None, "row", None, "col"))
    return jax.shard_map(
        on_device,
        mesh=mesh,
        in_specs=placed,
        out_specs=P(None, "row", None, None, "col", None),
        check_vma=False,
    )
```

```python
import jax
import jax.numpy as jnp
from jax import lax
from jax.experimental import pallas as pl
from jax.experimental.pallas import tpu as pltpu
from jax.sharding import PartitionSpec as P

W = 256
NB = 32
HIGHEST = lax.Precision.HIGHEST
F32 = jnp.float32
BF16 = jnp.bfloat16


def dot_nn(a, b):
    return lax.dot_general(a, b, (((1,), (0,)), ((), ())), precision=HIGHEST, preferred_element_type=F32)


def dot_nt(a, b):
    return lax.dot_general(a, b, (((1,), (1,)), ((), ())), precision=HIGHEST, preferred_element_type=F32)


def dot_tn(a, b):
    return lax.dot_general(a, b, (((0,), (0,)), ((), ())), precision=HIGHEST, preferred_element_type=F32)


def split3(x):
    hi = x.astype(BF16)
    rest = x - hi.astype(F32)
    mid = rest.astype(BF16)
    low = (rest - mid.astype(F32)).astype(BF16)
    return hi, mid, low


def eliminate(rows):
    sub = lax.broadcasted_iota(jnp.int32, (8, 384), 0)
    for t in range(4):
        x = rows[t]
        head = x[:, 0:128]
        cols = [jnp.broadcast_to(head[:, 8 * t + k : 8 * t + k + 1], (8, 128)) for k in range(8)]
        below = {
            g: [
                jnp.broadcast_to(rows[g][:, 8 * t + k : 8 * t + k + 1], (8, 128))
                for k in range(8)
            ]
            for g in range(t + 1, 4)
        }
        a = {
            (i, k): jnp.broadcast_to(cols[k][i : i + 1, :], (8, 128))
            for k in range(8)
            for i in range(k, 8)
        }
        r = [jnp.broadcast_to(x[k : k + 1, :], (8, 384)) for k in range(8)]
        for k in range(8):
            scale = lax.rsqrt(a[k, k])
            wide = jnp.concatenate([scale] * 3, axis=1)
            r[k] = r[k] * wide
            for g in below:
                below[g][k] = below[g][k] * scale
            l = {i: a[i, k] * scale for i in range(k + 1, 8)}
            for i in range(k + 1, 8):
                for j in range(k + 1, i + 1):
                    a[i, j] = a[i, j] - l[i] * l[j]
                r[i] = r[i] - jnp.concatenate([l[i]] * 3, axis=1) * r[k]
                for g in below:
                    below[g][i] = below[g][i] - l[i] * below[g][k]
        out = r[0]
        for k in range(1, 8):
            out = jnp.where(sub == k, r[k], out)
        rows[t] = out
        for g in below:
            acc = rows[g]
            for k in range(8):
                acc = acc - jnp.concatenate([below[g][k]] * 3, axis=1) * r[k]
            rows[g] = acc
    return rows


def factor_block(g_ref, u_ref, v_ref, beside=None):
    lane = lax.broadcasted_iota(jnp.int32, (NB, W), 1)
    row = lax.broadcasted_iota(jnp.int32, (NB, W), 0)
    eye = (
        lax.broadcasted_iota(jnp.int32, (NB, 128), 0)
        == lax.broadcasted_iota(jnp.int32, (NB, 128), 1)
    ).astype(F32)
    tail = lax.broadcasted_iota(jnp.int32, (W - NB, W), 1)

    def panel(p, carry):
        if beside is not None:
            beside(p)
        x = jnp.concatenate([g_ref[0:NB, :], eye], axis=1)
        rows = eliminate([x[8 * t : 8 * t + 8] for t in range(4)])
        r = jnp.concatenate(rows, axis=0)
        shifted = pltpu.roll(r, 384 - NB, 1)[:, 0:W]
        at = pl.multiple_of(p * NB, NB)
        u_ref[pl.ds(at, NB), :] = jnp.where(
            lane >= row + at, pltpu.roll(r[:, 0:W], at, 1), 0.0
        )
        v_ref[pl.ds(at, NB), :] = jnp.where(
            lane <= row + at, pltpu.roll(shifted, at + NB, 1), 0.0
        )
        hi, mid, low = split3(shifted)
        left = jnp.concatenate([hi, hi, mid, mid, hi, low], axis=0)
        right = jnp.concatenate([hi, mid, hi, mid, low, hi], axis=0)
        prod = lax.dot_general(
            left, right, (((0,), (0,)), ((), ())), preferred_element_type=F32
        )
        old = pltpu.roll(g_ref[NB:W, :], W - NB, 1)
        g_ref[0 : W - NB, :] = jnp.where(tail < W - NB, old, 0.0) - prod[0 : W - NB, :]
        return carry

    lax.fori_loop(0, W // NB, panel, 0)


H = W // 2
PACKED = H + 16
PIECE = PACKED // 2


def half_masks():
    return (
        lax.broadcasted_iota(jnp.int32, (H, H), 0),
        lax.broadcasted_iota(jnp.int32, (H, H), 1),
    )


def unpack(packed):
    below, right = half_masks()
    mixed = packed[0:H, 0:H]
    flipped = jnp.transpose(mixed)
    first = jnp.where(below >= right, mixed, flipped)
    second = jnp.where(below < right, mixed, flipped)
    second = jnp.where(below == right, packed[H : H + 1, 0:H], second)
    corner = packed[0:H, H:W]
    top = jnp.concatenate([first, jnp.transpose(corner)], axis=1)
    return jnp.concatenate([top, jnp.concatenate([corner, second], axis=1)], axis=0)


def factor_kernel(
    mine_ref, other_ref, slab_ref, twin_ref,
    panel_ref, row_ref, g_ref, u_ref, v0_ref, v1_ref, r0_ref, r1_ref,
):
    r, c = lax.axis_index("row"), lax.axis_index("col")
    even = lax.rem(c, 2) == 0

    def joined(t, side):
        spots = [lax.rem(x - r // 8 + 4, 4) for x in range(4)]
        tall = [
            jnp.where(even == side, mine_ref[spot, t], other_ref[spot, t]) for spot in spots
        ]
        return jnp.concatenate(
            [jnp.concatenate(tall[2 * h : 2 * h + 2], axis=0) for h in range(2)], axis=1
        )

    g_ref[...] = unpack(joined(0, True))
    factor_block(g_ref, u_ref, v0_ref)
    upper, lower = joined(0, False), joined(1, True)
    low = jnp.concatenate(
        [jnp.transpose(lower[0:H, 0:H]), jnp.transpose(lower[0:H, H:W])], axis=1
    )
    a01 = jnp.concatenate([upper[0:H], low], axis=0)
    v0 = v0_ref[...]
    pt = dot_nn(v0, a01)
    g_ref[...] = unpack(joined(1, False)) - dot_tn(pt, pt)
    first_u = jnp.transpose(u_ref[...])
    for s, ref in enumerate((r0_ref, r1_ref)):
        for m in range(2):
            for h in range(2):
                i = 2 * m + h
                ref[m * W : m * W + W, h * H : h * H + H] = jnp.where(
                    even == (s == 0), slab_ref[i], twin_ref[i]
                )

    def beside(p):
        span = pl.ds(pl.multiple_of(p * 64, 64), 64)
        first = dot_nt(r0_ref[span, :], v0_ref[...])
        panel_ref[span, :] = first
        r1_ref[span, :] = r1_ref[span, :] - dot_nn(first, pt)
        r0_ref[span, :] = dot_nn(first, v0_ref[...])

    factor_block(g_ref, u_ref, v1_ref, beside)
    v1 = v1_ref[...]
    p10v0 = dot_tn(pt, v0)
    second = dot_nt(r1_ref[...], v1)
    back1 = dot_nn(second, v1)
    row_ref[:, 0:W] = r0_ref[...] - dot_nn(back1, p10v0)
    row_ref[:, W : 2 * W] = back1

    @pl.when(c != 0)
    def _():
        panel_ref[...] = second

    @pl.when(r == 0)
    def _():
        row_ref[0:W, 0:W] = -v0
        row_ref[0:W, W : 2 * W] = jnp.zeros((W, W), F32)
        panel_ref[0:W, :] = jnp.where(c == 0, first_u, pt)

    @pl.when(r == 1)
    def _():
        row_ref[0:W, 0:W] = dot_nn(v1, p10v0)
        row_ref[0:W, W : 2 * W] = -v1
        panel_ref[0:W, :] = jnp.transpose(jnp.where(c == 0, pt, u_ref[...]))


def factor_pair(mine, other, slab, twin):
    return pl.pallas_call(
        factor_kernel,
        out_shape=[
            jax.ShapeDtypeStruct((2 * W, W), F32),
            jax.ShapeDtypeStruct((2 * W, 2 * W), F32),
        ],
        scratch_shapes=[pltpu.VMEM((W, W), F32)] * 4
        + [pltpu.VMEM((2 * W, W), F32)] * 2,
        compiler_params=pltpu.CompilerParams(vmem_limit_bytes=24 * 1024 * 1024),
        name="factor_pair",
    )(mine, other, slab, twin)


def extract_kernel(pattern_ref, front_ref, slab_ref, packed_ref, *piece_refs):
    r, c = lax.axis_index("row"), lax.axis_index("col")
    parts = []
    for m in range(2):
        keep = pattern_ref[m, 0] > 0
        for h in range(2):
            part = jnp.where(keep, front_ref[m * W : m * W + W, h, :], 0.0)
            slab_ref[2 * m + h] = part
            piece_refs[2 * m + h][...] = part
            parts.append(part)
    below, right = half_masks()

    def put(first, second, extra):
        packed_ref[...] = jnp.concatenate(
            [first, jnp.broadcast_to(extra, (PACKED - H, H)), second, jnp.zeros((PACKED - H, H), F32)],
            axis=0,
        )

    @pl.when(r == c)
    def _():
        second = parts[1][H:W]
        diagonal = jnp.sum(jnp.where(below == right, second, 0.0), axis=0, keepdims=True)
        put(jnp.where(below >= right, parts[0][0:H], second), parts[0][H:W], diagonal)

    zero = jnp.zeros((1, H), F32)

    @pl.when(r < c)
    def _():
        put(parts[0][0:H], parts[1][0:H], zero)

    @pl.when(r > c)
    def _():
        put(parts[1][0:H], parts[1][H:W], zero)


def extract(pattern, view):
    return pl.pallas_call(
        extract_kernel,
        grid=(1,),
        in_specs=[
            pl.BlockSpec(memory_space=pltpu.SMEM),
            pl.BlockSpec((2 * W, 8, 128), lambda i: (0, 0, 0)),
        ],
        out_specs=[pl.BlockSpec(memory_space=pltpu.VMEM)] * 6,
        out_shape=[
            jax.ShapeDtypeStruct((4, W, 128), F32),
            jax.ShapeDtypeStruct((2 * PACKED, H), F32),
        ]
        + [jax.ShapeDtypeStruct((W, 128), F32)] * 4,
        compiler_params=pltpu.CompilerParams(vmem_limit_bytes=56 * 1024 * 1024),
        name="extract",
    )(pattern, view)


FAR = ((0, 1, 7, 2), (4, 3, 5, 6))


def update_kernel(
    pattern_ref, front_hbm, q_hbm, panel_ref, row_ref, out_hbm,
    front_ref, q_ref, out_ref, front_sem, q_sem, out_sem,
):
    r, c = lax.axis_index("row"), lax.axis_index("col")
    x = r // 8
    q_copies, front_copies, out_copies = [], [], []

    def begin(source, target, sem):
        copy = pltpu.make_async_copy(source, target, sem)
        copy.start()
        return copy

    for m in range(2):
        for h in range(2):
            for s in range(2):
                i = 4 * m + 2 * h + s
                at = lax.rem(c + FAR[s][2 * m + h], 8)
                q_copies.append(begin(q_hbm.at[at], q_ref.at[i], q_sem.at[i]))
    for m in range(2):
        half = pl.ds(m * 4096, 4096)
        front_copies.append(begin(front_hbm.at[half], front_ref.at[half], front_sem.at[m]))
        out_copies.append(
            pltpu.make_async_copy(out_ref.at[half], out_hbm.at[half], out_sem.at[m])
        )
    for m in range(2):
        place = r + 32 * m
        row = row_ref[m * W : m * W + W, :]
        scale, parts = [], []
        for n in range(8):
            if m == 0 and n % 4 == 0:
                for copy in q_copies[n : n + 4]:
                    copy.wait()
            j = 4 * (n // 4)
            near = lax.rem(n % 4 - x + 4, 4)
            raw = jnp.concatenate([q_ref[j + i, near] for i in (0, 2, 1, 3)], axis=1)
            prod = dot_nt(row, raw)
            keep = jnp.logical_and(
                pattern_ref[m, n] > 0, jnp.logical_and(place > 1, c + 8 * n > 1)
            )
            parts += [prod[:, 0:128], prod[:, 128:256]]
            scale.append(jnp.broadcast_to(jnp.where(keep, 1.0, 0.0), (2, 128)))
        scale = jnp.concatenate(scale, axis=0)[None]
        moved = jnp.swapaxes(jnp.stack(parts), 0, 1)
        half = pl.ds(4096 * m, 4096)
        front_copies[m].wait()
        old = front_ref[half, :].reshape(W, 16, 128)
        out_ref[half, :] = (old * scale - moved).reshape(4096, 128)

        @pl.when(c < 2)
        def _():
            for h in range(2):
                out_ref[pl.ds(4096 * m + h, W, stride=16), :] = panel_ref[
                    m * W : m * W + W, 128 * h : 128 * h + 128
                ]

        out_copies[m].start()
    for copy in out_copies:
        copy.wait()


def update(pattern, view, gathered, panel, row):
    hbm = pl.BlockSpec(memory_space=pl.ANY)
    vmem = pl.BlockSpec(memory_space=pltpu.VMEM)
    return pl.pallas_call(
        update_kernel,
        in_specs=[pl.BlockSpec(memory_space=pltpu.SMEM), hbm, hbm, vmem, vmem],
        out_specs=hbm,
        out_shape=jax.ShapeDtypeStruct((8192, 128), F32),
        scratch_shapes=[
            pltpu.VMEM((8192, 128), F32),
            pltpu.VMEM((8, 4, W, 128), F32),
            pltpu.VMEM((8192, 128), F32),
            pltpu.SemaphoreType.DMA((2,)),
            pltpu.SemaphoreType.DMA((8,)),
            pltpu.SemaphoreType.DMA((2,)),
        ],
        compiler_params=pltpu.CompilerParams(vmem_limit_bytes=52 * 1024 * 1024),
        name="update",
    )(pattern, view, gathered, panel, row)


BOTH = ("row", "col")


def device(x, z, c):
    return (x * 8 + z) * 8 + c


def around(value, axis, moves):
    return [lax.ppermute(value, axis, pairs) for pairs in moves]


def on_device(front, pattern):
    row_place = lax.axis_index("row")
    col_place = lax.axis_index("col")
    view = front.reshape(8192, 128)
    present = pattern.reshape(2, 8)
    slab, packed, *pieces = extract(present, front.reshape(512, 16, 128))

    x_moves = [
        [(((x + d) % 4) * 8 + z, x * 8 + z) for x in range(4) for z in range(8)]
        for d in (1, 2, 3)
    ]
    swap = [(c, c ^ 1) for c in range(8)]
    groups = [[x * 8 + z for z in range(8)] for x in range(4)]

    across = lax.all_gather(packed, "col")
    held = jnp.where(col_place % 2 == 0, across[0], across[1])

    share = 0.0
    for k in range(4):
        pairs = [
            (device(x, z, s), device(x, (z + FAR[s][k]) % 8, z))
            for x in range(4)
            for z in range(8)
            for s in range(2)
        ]
        share = share + lax.ppermute(pieces[k], BOTH, pairs)
    line = jnp.stack([share] + around(share, "row", x_moves))
    moved = lax.ppermute(slab, "col", [(0, 6), (1, 7)])
    line, moved = lax.optimization_barrier((line, moved))
    gathered = lax.all_gather(line, "row", axis_index_groups=groups)
    slab = jnp.where(col_place < 2, slab, moved)

    quarters = [held[PIECE * x : PIECE * x + PIECE] for x in range(4)]
    held = jnp.where(row_place < 2, quarters[0], 0.0)
    for x in (1, 3, 2):
        held = held + lax.ppermute(quarters[x], "row", [(z, x * 8 + z) for z in range(2)])
    start = held
    moved = lax.ppermute(slab, "col", [(0, 2), (1, 3), (6, 4), (7, 5)])

    for d in (2, 6, 4):
        held = held + lax.ppermute(start, "row", [
            (x * 8 + z, x * 8 + (z + d) % 8) for x in range(4) for z in range(2)
        ])
    after = lax.ppermute(held, "row", [
        (x * 8 + z, x * 8 + (z + 1) % 8) for x in range(4) for z in range(8)
    ])
    even = row_place % 2 == 0
    diag = jnp.stack([jnp.where(even, held, after), jnp.where(even, after, held)])
    slab = jnp.where((col_place < 2) | (col_place > 5), slab, moved)
    diag, slab = lax.optimization_barrier((diag, slab))
    twin = lax.ppermute(slab, "col", swap)
    mine = jnp.stack([diag] + around(diag, "row", x_moves))
    other = lax.ppermute(mine, "col", swap)

    panel, row = factor_pair(mine, other, slab, twin)
    out = update(present, view, gathered, panel, row)
    return out.reshape(2, 1, 256, 8, 1, 256)


def solution(mesh):
    placed = (P(None, "row", None, None, "col", None), P(None, "row", None, "col"))
    return jax.shard_map(
        on_device,
        mesh=mesh,
        in_specs=placed,
        out_specs=P(None, "row", None, None, "col", None),
        check_vma=False,
    )
```
